256 devices in a mesh: row: 16 (over z, x_hi), col: 4 (over y), depth: 4 (over x_lo, core).
Axes of the slice: x: 4 (x_hi: 2, x_lo: 2; x = x_hi * 2 + x_lo), y: 4, z: 8, core: 2. Of those that a mesh axis runs over, the one named last changes fastest.
Arguments:
- inputs: bfloat16 [1536, 12288], P('depth', 'row'), may hold values from -6 to 6
- up_weight: bfloat16 [12288, 24576], P('row', 'col'), may hold values from -0.078125 to 0.078125
- grad_hidden: bfloat16 [1536, 24576], P('depth', ('col', 'row')), may hold values from -16 to 16
Outputs:
- grad_inputs: bfloat16 [1536, 12288], P('depth', 'row')
- grad_weight: bfloat16 [12288, 24576], P('row', ('col', 'depth'))
The draws below stay inside these ranges and needn't reach their ends.
All inputs are finite; a program needn't handle non-finite values.
Results may differ from the reference program's by a relative error of at most 0.005.
Values may be sent and summed in bfloat16 or wider, within the bound.
No kernel may reach another device: no remote copies, remote signals or barrier semaphores. Data moves between devices by JAX's collectives and lax.ppermute only.
A program may use at most 128 MiB of HBM per device.

```python
import math
import jax
import jax.numpy as jnp
from jax import lax

D = 12288
FF = 24576
TOKENS = 1536


def raised(drawn, key, source, target, blocks, factor):
    def block_of(axis_at):
        return (jnp.arange(drawn.shape[axis_at]) // (drawn.shape[axis_at] // blocks)).reshape((-1,) + (1,) * (drawn.ndim - 1 - axis_at))

    first = jax.random.permutation(key, blocks)[block_of(target)]
    far = (block_of(target) + blocks // 2) % blocks
    return jnp.where((block_of(source) == first) | (block_of(source) == far), factor * drawn, drawn)


def block_scale(own_key, extent, pieces, low, largest):
    def one(position, shards_of):
        heights = jax.random.uniform(jax.random.fold_in(jax.random.fold_in(own_key, 6), position), (shards_of,), jnp.float32, low / len(pieces), largest / len(pieces))
        return jnp.repeat(jnp.exp(heights), extent[position] // shards_of).reshape((-1,) + (1,) * (len(extent) - position - 1))

    level = one(*pieces[0])
    for cut in pieces[1:]:
        level = level * one(*cut)
    return level


def gaussian(own_key, shape, deviation, bound, cuts=(), held_as=jnp.bfloat16):
    gain = block_scale(own_key, shape, cuts, -0.22, 0.18) if cuts else 1.0
    result = jax.random.normal(own_key, shape, jnp.float32) * deviation * gain
    return jnp.minimum(jnp.maximum(result, -bound), bound).astype(held_as)


def heavy_noise(own_key, shape, scale, bound, cuts, heavy, dtype=jnp.bfloat16):
    drawn = scale * jax.random.normal(own_key, shape, jnp.float32)
    if cuts:
        drawn = drawn * block_scale(own_key, shape, cuts, -0.22, 0.18)
    return jnp.clip(raised(drawn, jax.random.fold_in(own_key, 3), *heavy), -bound, bound).astype(dtype)


def setup_inputs(seed: int = 0) -> dict:
    keys = jax.random.split(jax.random.key(seed), 4)
    return {
        "inputs": gaussian(keys[0], (TOKENS, D), 1.0, 6.0, ((0, 4), (1, 16))),
        "up_weight": heavy_noise(keys[1], (D, FF), D ** -0.5, 0.078125, ((0, 16), (1, 4)), (0, 1, 16, 2.0)),
        "grad_hidden": heavy_noise(keys[2], (TOKENS, FF), 1.0, 16.0, ((0, 4), (1, 64)), (0, 1, 64, 4.0)),
    }


GELU_FACTOR = math.sqrt(2.0 / math.pi)
GELU_CUBIC = 0.044715

def gelu_slope(values):
    argument = GELU_FACTOR * (values + GELU_CUBIC * values * values * values)
    tangent = jnp.tanh(argument)
    return 0.5 * (1.0 + tangent) + 0.5 * values * (1.0 - tangent * tangent) * GELU_FACTOR * (1.0 + 3.0 * GELU_CUBIC * values * values)

def reference(inputs, up_weight, grad_hidden):
    preact = jnp.dot(inputs, up_weight, preferred_element_type=jnp.float32)
    grad_preact = (grad_hidden.astype(jnp.float32) * gelu_slope(preact)).astype(jnp.bfloat16)
    grad_inputs = lax.dot_general(grad_preact, up_weight, (((1,), (1,)), ((), ())), preferred_element_type=jnp.float32).astype(jnp.bfloat16)
    grad_weight = lax.dot_general(inputs, grad_preact, (((0,), (0,)), ((), ())), preferred_element_type=jnp.float32).astype(jnp.bfloat16)
    return (grad_inputs, grad_weight)
```

```python
import math

import jax
import jax.numpy as jnp
from jax import lax
from jax.sharding import PartitionSpec as P

GELU_FACTOR = math.sqrt(2.0 / math.pi)
GELU_CUBIC = 0.044715

ROWS, COLS, DEPTHS = 16, 4, 4
RING = 8
AXES = ("row", "col", "depth")


def gelu_slope(values):
    argument = GELU_FACTOR * (values + GELU_CUBIC * values * values * values)
    tangent = jnp.tanh(argument)
    return 0.5 * (1.0 + tangent) + 0.5 * values * (1.0 - tangent * tangent) * GELU_FACTOR * (
        1.0 + 3.0 * GELU_CUBIC * values * values
    )


def send(x, target):
    perm = []
    for r in range(ROWS):
        for c in range(COLS):
            for d in range(DEPTHS):
                tz, th, tc, td = target(r // 2, r % 2, c, d)
                dst = (((tz % RING) * 2 + th) * COLS + tc % COLS) * DEPTHS + td
                perm.append(((r * COLS + c) * DEPTHS + d, dst))
    return lax.ppermute(x, AXES, perm)


def along_z(x, step, cross=False):
    return send(x, lambda z, h, y, d: (z + step, h ^ int(cross), y, d))


def other_half(x):
    return send(x, lambda z, h, y, d: (z, 1 - h, y, d))


def along_y(x, step):
    return send(x, lambda z, h, y, d: (z, h, y + step, d))


def along_depth(x, mask):
    return send(x, lambda z, h, y, d: (z, h, y, d ^ mask))


def rolled(x, shift):
    n = x.shape[0]
    return lax.dynamic_slice_in_dim(jnp.concatenate([x, x]), shift, n, 0)


def matmul(a, b, dims):
    return lax.dot_general(a, b, (dims, ((), ())), preferred_element_type=jnp.float32)


EARLY = (0, 1, 7, 2)
LATE = (6, 3, 5, 4)
ALL = tuple(k for pair in zip(EARLY, LATE) for k in pair)


def body(inputs, up_weight, grad_hidden):
    row, col, depth = (lax.axis_index(name) for name in AXES)
    z, half = row // 2, row % 2
    tokens, width = inputs.shape
    part = tokens // RING
    hidden = up_weight.shape[1] // DEPTHS
    block = hidden // 4
    f32, bf16 = jnp.float32, jnp.bfloat16

    x_own = rolled(inputs.reshape(RING, part, width), z)
    x_core = along_depth(x_own, 1)
    x_next = along_depth(x_own, 2)
    x_far = along_depth(x_next, 1)

    piece = (depth ^ (row // 4)) // 2 * 4 + row % 4
    pieces = rolled(grad_hidden.reshape(RING, part, block), piece)
    came = []
    for q in range(RING):

        def owner(zz, h, y, d, q=q):
            r = zz * 2 + h
            target = r // 4
            return ((d ^ target) // 2 * 4 + r % 4 + q, (d ^ target) % 2, y, target)

        came.append(send(pieces[q], owner))
    gates = rolled(jnp.stack(came[::-1]), RING - 1 - z)

    weight = lax.dynamic_slice_in_dim(up_weight, depth * hidden, hidden, 1)

    def ordered(a, b):
        return jnp.where(half == 0, jnp.stack([a, b]), jnp.stack([b, a]))

    streams = []
    for s, (a, b) in enumerate(((x_own, x_core), (x_next, x_far))):
        x = ordered(a, b)

        def partial(k):
            return matmul(x[:, k].reshape(2 * part, width), weight, ((1,), (0,)))

        far = partial(4).astype(bf16)
        up = along_z(far[:part], 1).astype(f32)
        down = along_z(far[part:], -1).astype(f32)
        nothing = jnp.zeros_like(up)
        up = jnp.concatenate([up, nothing])
        down = jnp.concatenate([nothing, down])
        for k in (3, 2):
            up = along_z((partial(k) + up).astype(bf16), 1).astype(f32)
            down = along_z((partial(RING - k) + down).astype(bf16), -1).astype(f32)
        home = partial(0)
        cross = other_half(home[part:].astype(bf16)).astype(f32)
        up = (partial(1) + up).astype(bf16)
        down = (partial(7) + down).astype(bf16)
        total = home[:part] + cross
        for sent, step in ((up, 1), (down, -1)):
            total = total + along_z(sent[:part], step).astype(f32)
            total = total + along_z(sent[part:], step, cross=True).astype(f32)
        gate = gates[4 * s : 4 * s + 4].transpose(1, 0, 2).reshape(part, hidden)
        grad = (gate.astype(f32) * gelu_slope(total)).astype(bf16)

        held = {0: (grad, other_half(grad))}
        held[7] = (along_z(grad, 1), along_z(grad, 1, cross=True))
        held[1] = (along_z(grad, -1), along_z(grad, -1, cross=True))
        for k in (1, 2):
            held[7 - k] = tuple(along_z(g, 1) for g in held[8 - k])
            held[k + 1] = tuple(along_z(g, -1) for g in held[k])
        held[4] = (along_z(held[5][0], 1), along_z(held[3][1], -1))
        streams.append((x, held))

    def summed(s, group):
        held = streams[s][1]
        grads = jnp.concatenate([held[k][i] for i in range(2) for k in group])
        result = matmul(grads, weight, ((1,), (1,))).astype(bf16).reshape(2, -1, width)
        share = result.shape[1] // COLS

        def piece_of(y):
            return lax.dynamic_slice_in_dim(result, y % COLS * share, share, 1)

        total = piece_of(col).astype(f32)
        for j in range(1, COLS):
            total = total + along_y(piece_of(col + j), j).astype(f32)
        total = total.astype(bf16)
        first = send(total[0], lambda zz, h, y, d: (zz, h, y, d ^ (2 * s + h)))
        second = send(total[1], lambda zz, h, y, d: (zz, h, y, d ^ (2 * s + 1 - h)))
        return first.astype(f32) + second.astype(f32), grads

    def chosen(s, group):
        x = streams[s][0]
        return jnp.concatenate([x[i, k] for i in range(2) for k in group])

    near, grads = summed(0, ALL)
    grad_weight = matmul(chosen(0, ALL), grads, ((0,), (0,)))
    near = near.reshape(2, part, width)
    found = [None] * RING
    for n, group in enumerate((EARLY, LATE)):
        far, grads = summed(1, group)
        grad_weight = grad_weight + matmul(chosen(1, group), grads, ((0,), (0,)))
        mine = (near[n] + far).astype(bf16)
        around = jnp.stack([mine] + [along_y(mine, -j) for j in range(1, COLS)])
        around = rolled(around, (COLS - col) % COLS)
        for y, k in enumerate(group):
            found[k] = around[y]
    grad_inputs = rolled(jnp.stack(found), (RING - z) % RING).reshape(tokens, width)
    return (grad_inputs, grad_weight.astype(bf16))


def solution(mesh):
    placed = (P("depth", "row"), P("row", "col"), P("depth", ("col", "row")))
    return jax.shard_map(
        body,
        mesh=mesh,
        in_specs=placed,
        out_specs=(P("depth", "row"), P("row", ("col", "depth"))),
        check_vma=False,
    )
```

```python
import math

import jax
import jax.numpy as jnp
from jax import lax
from jax.sharding import PartitionSpec as P

GELU_FACTOR = math.sqrt(2.0 / math.pi)
GELU_CUBIC = 0.044715

ROWS, COLS, DEPTHS = 16, 4, 4
RING = 8
AXES = ("row", "col", "depth")


def gelu_slope(values):
    argument = GELU_FACTOR * (values + GELU_CUBIC * values * values * values)
    tangent = jnp.tanh(argument)
    return 0.5 * (1.0 + tangent) + 0.5 * values * (1.0 - tangent * tangent) * GELU_FACTOR * (
        1.0 + 3.0 * GELU_CUBIC * values * values
    )


def send(x, target):
    perm = []
    for r in range(ROWS):
        for c in range(COLS):
            for d in range(DEPTHS):
                tz, th, tc, td = target(r // 2, r % 2, c, d)
                dst = (((tz % RING) * 2 + th) * COLS + tc % COLS) * DEPTHS + td
                perm.append(((r * COLS + c) * DEPTHS + d, dst))
    return lax.ppermute(x, AXES, perm)


def along_z(x, step, cross=False):
    return send(x, lambda z, h, y, d: (z + step, h ^ int(cross), y, d))


def other_half(x):
    return send(x, lambda z, h, y, d: (z, 1 - h, y, d))


def along_y(x, step):
    return send(x, lambda z, h, y, d: (z, h, y + step, d))


def along_depth(x, mask):
    return send(x, lambda z, h, y, d: (z, h, y, d ^ mask))


def rolled(x, shift):
    n = x.shape[0]
    return lax.dynamic_slice_in_dim(jnp.concatenate([x, x]), shift, n, 0)


def matmul(a, b, dims):
    return lax.dot_general(a, b, (dims, ((), ())), preferred_element_type=jnp.float32)


EARLY = (0, 1, 7, 2)
LATE = (6, 3, 5, 4)
ALL = tuple(k for pair in zip(EARLY, LATE) for k in pair)


def body(inputs, up_weight, grad_hidden):
    row, col, depth = (lax.axis_index(name) for name in AXES)
    z, half = row // 2, row % 2
    tokens, width = inputs.shape
    part = tokens // ROWS
    hidden = up_weight.shape[1] // DEPTHS
    f32, bf16 = jnp.float32, jnp.bfloat16

    x_own = inputs.reshape(RING, 2, part, width)
    x_own = rolled(jnp.where(half == 0, x_own, x_own[:, ::-1]), z)
    x_core = along_depth(x_own, 1)
    x_next = along_depth(x_own, 2)
    x_far = along_depth(x_next, 1)
    x_blocks = (x_own, x_core, x_next, x_far)

    came = lax.all_to_all(grad_hidden.reshape(ROWS, part, hidden // 4), "row", 0, 0)
    came = came.reshape(4, 4, part, hidden // 4)
    gates = []
    for m in range(DEPTHS):
        gate = lax.dynamic_index_in_dim(came, depth ^ m, 0, keepdims=False)
        gate = along_depth(gate, m) if m else gate
        gates.append(gate.transpose(1, 0, 2).reshape(part, hidden))

    weight = lax.dynamic_slice_in_dim(up_weight, depth * hidden, hidden, 1)

    slot = 2 * part
    streams = []
    for s in range(2):
        x = jnp.stack(x_blocks[2 * s : 2 * s + 2], axis=2).reshape(RING, 2 * slot, width)

        def partial(k):
            return matmul(x[k], weight, ((1,), (0,)))

        far = partial(4).astype(bf16)
        up = along_z(far[:slot], 1).astype(f32)
        down = along_z(far[slot:], -1).astype(f32)
        nothing = jnp.zeros_like(up)
        up = jnp.concatenate([up, nothing])
        down = jnp.concatenate([nothing, down])
        for k in (3, 2, 1):
            up = along_z((partial(k) + up).astype(bf16), 1).astype(f32)
            down = along_z((partial(RING - k) + down).astype(bf16), -1).astype(f32)
        total = partial(0) + up + down
        total = total[:slot] + other_half(total[slot:].astype(bf16)).astype(f32)
        gate = jnp.concatenate(gates[2 * s : 2 * s + 2])
        grad = (gate.astype(f32) * gelu_slope(total)).astype(bf16)

        both = jnp.concatenate([grad, other_half(grad)])
        held = {0: both}
        up, down = both, both
        for k in (1, 2, 3):
            held[RING - k] = up = along_z(up, 1)
            held[k] = down = along_z(down, -1)
        held[4] = jnp.concatenate([along_z(up[:slot], 1), along_z(down[slot:], -1)])
        streams.append((x, held))

    def summed(s, group):
        grads = jnp.concatenate([streams[s][1][k] for k in group])
        result = matmul(grads, weight, ((1,), (1,))).astype(bf16)
        share = result.shape[0] // COLS

        def piece_of(y):
            return lax.dynamic_slice_in_dim(result, y % COLS * share, share, 0)

        total = piece_of(col).astype(f32)
        for j in range(1, COLS):
            total = total + along_y(piece_of(col + j), j).astype(f32)
        total = total.astype(bf16).reshape(-1, 2, 2, part, width)
        total = [total[:, :, m] for m in range(2)]
        total = [along_depth(t, 2 * s + m) if s or m else t for m, t in enumerate(total)]
        return total[0].astype(f32) + total[1].astype(f32), grads

    def chosen(s, group):
        return jnp.concatenate([streams[s][0][k] for k in group])

    near, grads = summed(0, ALL)
    grad_weight = matmul(chosen(0, ALL), grads, ((0,), (0,)))
    found = [None] * RING
    for n, group in enumerate((EARLY, LATE)):
        far, grads = summed(1, group)
        grad_weight = grad_weight + matmul(chosen(1, group), grads, ((0,), (0,)))
        mine = (near[n] + far[0]).astype(bf16)
        around = jnp.stack([mine] + [along_y(mine, -j) for j in range(1, COLS)])
        around = rolled(around, (COLS - col) % COLS)
        for y, k in enumerate(group):
            found[k] = around[y]
    result = rolled(jnp.stack(found), (RING - z) % RING)
    result = jnp.where(half == 0, result, result[:, ::-1])
    return (result.reshape(tokens, width), grad_weight.astype(bf16))


def solution(mesh):
    placed = (P("depth", "row"), P("row", "col"), P("depth", ("col", "row")))
    return jax.shard_map(
        body,
        mesh=mesh,
        in_specs=placed,
        out_specs=(P("depth", "row"), P("row", ("col", "depth"))),
        check_vma=False,
    )
```

```python
import math

import jax
import jax.numpy as jnp
from jax import lax
from jax.sharding import PartitionSpec as P

GELU_FACTOR = math.sqrt(2.0 / math.pi)
GELU_CUBIC = 0.044715

ROWS, COLS, DEPTHS = 16, 4, 4
RING = 8
AXES = ("row", "col", "depth")


def gelu_slope(values):
    argument = GELU_FACTOR * (values + GELU_CUBIC * values * values * values)
    tangent = jnp.tanh(argument)
    return 0.5 * (1.0 + tangent) + 0.5 * values * (1.0 - tangent * tangent) * GELU_FACTOR * (
        1.0 + 3.0 * GELU_CUBIC * values * values
    )


def send(x, target):
    perm = []
    for r in range(ROWS):
        for c in range(COLS):
            for d in range(DEPTHS):
                tz, th, tc, td = target(r // 2, r % 2, c, d)
                dst = (((tz % RING) * 2 + th) * COLS + tc % COLS) * DEPTHS + td
                perm.append(((r * COLS + c) * DEPTHS + d, dst))
    return lax.ppermute(x, AXES, perm)


def along_z(x, step, cross=False):
    return send(x, lambda z, h, y, d: (z + step, h ^ int(cross), y, d))


def other_half(x):
    return send(x, lambda z, h, y, d: (z, 1 - h, y, d))


def along_y(x, step):
    return send(x, lambda z, h, y, d: (z, h, y + step, d))


def along_depth(x, mask):
    return send(x, lambda z, h, y, d: (z, h, y, d ^ mask))


def rolled(x, shift):
    n = x.shape[0]
    return lax.dynamic_slice_in_dim(jnp.concatenate([x, x]), shift, n, 0)


def matmul(a, b, dims):
    return lax.dot_general(a, b, (dims, ((), ())), preferred_element_type=jnp.float32)


def after(x, *others):
    return lax.optimization_barrier((x, *others))[0]


EARLY = (0, 1, 7, 2)
LATE = (6, 3, 5, 4)


def body(inputs, up_weight, grad_hidden):
    row, col, depth = (lax.axis_index(name) for name in AXES)
    z, half = row // 2, row % 2
    tokens, width = inputs.shape
    part = tokens // ROWS
    slot = 2 * part
    hidden = up_weight.shape[1] // DEPTHS
    f32, bf16 = jnp.float32, jnp.bfloat16

    x_own = inputs.reshape(RING, 2, part, width)
    x_own = rolled(jnp.where(half == 0, x_own, x_own[:, ::-1]), z)
    x_core = along_depth(x_own, 1)
    x_next = along_depth(x_own, 2)
    weight = lax.dynamic_slice_in_dim(up_weight, depth * hidden, hidden, 1)

    class Stream:
        def __init__(self, s, first, second):
            self.s = s
            self.x = jnp.stack([first, second], axis=2).reshape(RING, 2 * slot, width)

        def partial(self, k):
            return matmul(self.x[k], weight, ((1,), (0,)))

        def scatter_first(self):
            far = self.partial(4).astype(bf16)
            up = along_z(far[:slot], 1).astype(f32)
            down = along_z(far[slot:], -1).astype(f32)
            nothing = jnp.zeros_like(up)
            self.up = jnp.concatenate([up, nothing])
            self.down = jnp.concatenate([nothing, down])
            return far

        def scatter(self, k):
            up = (self.partial(k) + self.up).astype(bf16)
            down = (self.partial(RING - k) + self.down).astype(bf16)
            self.up = along_z(up, 1).astype(f32)
            self.down = along_z(down, -1).astype(f32)
            return up, down

        def slope(self, gates):
            total = self.partial(0) + self.up + self.down
            total = total[:slot] + other_half(total[slot:].astype(bf16)).astype(f32)
            gate = jnp.concatenate(gates)
            grad = (gate.astype(f32) * gelu_slope(total)).astype(bf16)
            both = jnp.concatenate([grad, other_half(grad)])
            self.held = {0: both}
            self.ahead = (both, both)

        def gather(self, k, *others):
            up, down = self.ahead
            if others:
                up, down = after(up, *others), after(down, *others)
            if k < 4:
                up, down = along_z(up, 1), along_z(down, -1)
                self.held[RING - k], self.held[k] = up, down
                self.ahead = (up, down)
            else:
                up, down = along_z(up[:slot], 1), along_z(down[slot:], -1)
                self.held[k] = jnp.concatenate([up, down])
                self.ahead = (up, down)

        def product(self, group, *others):
            held = [self.held[k] for k in group]
            grads = jnp.concatenate([after(held[0], *others)] + held[1:])
            result = matmul(grads, weight, ((1,), (1,))).astype(bf16)
            share = result.shape[0] // COLS

            def piece_of(y):
                return lax.dynamic_slice_in_dim(result, y % COLS * share, share, 0)

            pieces = [piece_of(col)] + [along_y(piece_of(col + j), j) for j in range(1, COLS)]
            return grads, pieces

        def over_depth(self, pieces, *others):
            pieces = [after(pieces[0], *others)] + pieces[1:]
            total = sum(p.astype(f32) for p in pieces).astype(bf16)
            total = total.reshape(2, 2, part, width)
            sent = [total[:, m] for m in range(2)]
            return [along_depth(t, 2 * self.s + m) if self.s or m else t for m, t in enumerate(sent)]

        def outer(self, group, grads, *others):
            x = jnp.concatenate([self.x[k] for k in group])
            return matmul(after(x, *others), grads, ((0,), (0,)))

    own = Stream(0, x_own, x_core)
    own.scatter_first()
    sent, _ = own.scatter(3)
    x_next = after(x_next, sent)
    x_far = along_depth(x_next, 1)
    nxt = Stream(1, x_next, x_far)
    first = nxt.scatter_first()
    sent, _ = own.scatter(2)

    grad_hidden = after(grad_hidden, first, sent)
    came = lax.all_to_all(grad_hidden.reshape(ROWS, part, hidden // 4), "row", 0, 0)
    nxt.scatter(3)
    sent, _ = own.scatter(1)
    came = after(came.reshape(4, 4, part, hidden // 4), sent)
    gates = []
    for m in range(DEPTHS):
        gate = lax.dynamic_index_in_dim(came, depth ^ m, 0, keepdims=False)
        gate = along_depth(gate, m) if m else gate
        gates.append(gate.transpose(1, 0, 2).reshape(part, hidden))
    nxt.scatter(2)
    nxt.scatter(1)
    own.slope(gates[:2])
    nxt.slope(gates[2:])

    own.gather(1)
    nxt.gather(1)
    nxt.gather(2)
    own.gather(2, *nxt.ahead[:1])
    nxt.gather(3)
    own.gather(3)
    nxt_grads_a, nxt_a = nxt.product(EARLY, own.held[2])
    nxt.gather(4)
    nxt_a = nxt.over_depth(nxt_a, nxt.held[3], nxt.held[5])
    outer = nxt.outer(EARLY, nxt_grads_a, nxt.held[3], nxt.held[5])
    own.gather(4)
    own_grads_a, own_a = own.product(EARLY, own.held[3], own.held[5])
    nxt_grads_b, nxt_b = nxt.product(LATE)
    own_a = own.over_depth(own_a, nxt.held[4])
    outer = outer + own.outer(EARLY, own_grads_a, nxt.held[4])
    own_grads_b, own_b = own.product(LATE)
    nxt_b = nxt.over_depth(nxt_b, own.held[4])
    own_b = own.over_depth(own_b)
    outer = outer + nxt.outer(LATE, nxt_grads_b, own.held[4])
    outer = outer + own.outer(LATE, own_grads_b)

    found = [None] * RING
    for group, parts in ((EARLY, own_a + nxt_a), (LATE, own_b + nxt_b)):
        mine = sum(p.astype(f32) for p in parts).astype(bf16)
        around = jnp.stack([mine] + [along_y(mine, -j) for j in range(1, COLS)])
        around = rolled(around, (COLS - col) % COLS)
        for y, k in enumerate(group):
            found[k] = around[y]
    result = rolled(jnp.stack(found), (RING - z) % RING)
    result = jnp.where(half == 0, result, result[:, ::-1])
    return (result.reshape(tokens, width), outer.astype(bf16))


def solution(mesh):
    placed = (P("depth", "row"), P("row", "col"), P("depth", ("col", "row")))
    return jax.shard_map(
        body,
        mesh=mesh,
        in_specs=placed,
        out_specs=(P("depth", "row"), P("row", ("col", "depth"))),
        check_vma=False,
    )
```

```python
import math

import jax
import jax.numpy as jnp
from jax import lax
from jax.sharding import PartitionSpec as P

GELU_FACTOR = math.sqrt(2.0 / math.pi)
GELU_CUBIC = 0.044715

ROWS, COLS, DEPTHS = 16, 4, 4
RING = 8
AXES = ("row", "col", "depth")


def gelu_slope(values):
    argument = GELU_FACTOR * (values + GELU_CUBIC * values * values * values)
    tangent = jnp.tanh(argument)
    return 0.5 * (1.0 + tangent) + 0.5 * values * (1.0 - tangent * tangent) * GELU_FACTOR * (
        1.0 + 3.0 * GELU_CUBIC * values * values
    )


def send(x, target):
    perm = []
    for r in range(ROWS):
        for c in range(COLS):
            for d in range(DEPTHS):
                tz, th, tc, td = target(r // 2, r % 2, c, d)
                dst = (((tz % RING) * 2 + th) * COLS + tc % COLS) * DEPTHS + td
                perm.append(((r * COLS + c) * DEPTHS + d, dst))
    return lax.ppermute(x, AXES, perm)


def along_ring(x, back=False):
    return send(x, lambda z, h, y, d: (z + (1 if d % 2 == int(back) else -1), h, y, d))


def other_half(x):
    return send(x, lambda z, h, y, d: (z, 1 - h, y, d))


def along_y(x, step):
    return send(x, lambda z, h, y, d: (z, h, y + step, d))


def along_depth(x, mask):
    return send(x, lambda z, h, y, d: (z, h, y, d ^ mask))


def other_core(x):
    return along_depth(x, 1)


def rolled(x, shift):
    n = x.shape[0]
    return lax.dynamic_slice_in_dim(jnp.concatenate([x, x]), shift, n, 0)


def matmul(a, b, dims):
    return lax.dot_general(a, b, (dims, ((), ())), preferred_element_type=jnp.float32)


def after(x, *others):
    return lax.optimization_barrier((x, *others))[0]


def body(inputs, up_weight, grad_hidden):
    row, col, depth = (lax.axis_index(name) for name in AXES)
    z, half, core = row // 2, row % 2, depth % 2
    tokens, width = inputs.shape
    part = tokens // ROWS
    slot = 2 * part
    hidden = up_weight.shape[1] // DEPTHS
    f32, bf16 = jnp.float32, jnp.bfloat16

    def swapped(x):
        return jnp.concatenate([x[i * part : (i + 1) * part] for i in (3, 2, 1, 0)])

    x = inputs.reshape(RING, 2, part, width)
    x = rolled(jnp.where(half == 0, x, x[:, ::-1]), z)
    x_up = x[:5]
    x_down = jnp.stack([x[-j % RING, ::-1] for j in range(5)])
    x_mine = jnp.where(core == 0, x_up, x_down)
    x_other = jnp.where(core == 0, x_down, x_up)
    x_core = other_core(x_other)
    x_next = along_depth(x_mine, 2)
    x_far = along_depth(x_other, 3)

    weight = lax.optimization_barrier(
        jnp.concatenate(
            [
                lax.dynamic_slice_in_dim(up_weight, (depth ^ m) * hidden, hidden, 1)
                for m in range(2)
            ],
            axis=1,
        )
    )

    class Stream:
        def __init__(self, first, second):
            x = jnp.stack([first, second], axis=2)
            self.x = [x[j].reshape(2 * slot, width) for j in range(5)]

        def scatter(self, j):
            if j == 4:
                sent = matmul(self.x[4][:slot], weight, ((1,), (0,))).astype(bf16)
                came = along_ring(sent).astype(f32)
                self.came = jnp.concatenate([came, jnp.zeros_like(came)])
            else:
                sent = matmul(self.x[j], weight, ((1,), (0,)))
                sent = (sent + self.came).astype(bf16)
                self.came = along_ring(sent).astype(f32)
            return sent

        def slope(self, gates):
            came = other_core(swapped(self.came[:, hidden:].astype(bf16))).astype(f32)
            total = matmul(self.x[0], weight[:, :hidden], ((1,), (0,)))
            total = total + self.came[:, :hidden] + came
            total = total[:slot] + other_half(total[slot:].astype(bf16)).astype(f32)
            gate = jnp.concatenate(gates)
            grad = (gate.astype(f32) * gelu_slope(total)).astype(bf16)
            both = jnp.concatenate([grad, other_half(grad)])
            ahead = jnp.concatenate([both, swapped(other_core(both))], axis=1)
            self.held = [ahead]

        def gather(self, *others):
            ahead = self.held[-1]
            if others:
                ahead = after(ahead, *others)
            if len(self.held) == 4:
                ahead = ahead[:slot]
            self.held.append(along_ring(ahead, back=True))

        def product(self, late, *others):
            if late:
                held = [self.held[0][:slot], self.held[3], self.held[4]]
                x = [self.x[0][:slot], self.x[3], self.x[4][:slot]]
            else:
                held, x = self.held[1:3], self.x[1:3]
            grads = jnp.concatenate([after(held[0], *others)] + held[1:])
            result = matmul(grads, weight, ((1,), (1,)))
            return jnp.concatenate(x), grads, result

    own = Stream(x_mine, x_core)
    own.scatter(4)
    sent = own.scatter(3)
    x_next, x_far = after(x_next, sent), after(x_far, sent)
    nxt = Stream(x_next, x_far)
    first = nxt.scatter(4)
    sent = own.scatter(2)

    grad_hidden = after(grad_hidden, first, sent).reshape(RING, 2, part, hidden // 4)
    grad_hidden = jnp.where(z // 2 % 2 == 0, grad_hidden, grad_hidden[:, ::-1])
    grad_hidden = grad_hidden.reshape(ROWS, part, hidden // 4)
    came = lax.all_to_all(grad_hidden, "row", 0, 0)
    nxt.scatter(3)
    sent = own.scatter(1)
    came = after(came.reshape(4, 4, part, hidden // 4), sent)
    gates = []
    for m in range(DEPTHS):
        gate = lax.dynamic_index_in_dim(came, depth ^ m, 0, keepdims=False)
        gate = along_depth(gate, m) if m else gate
        gates.append(gate.transpose(1, 0, 2).reshape(part, hidden))
    nxt.scatter(2)
    nxt.scatter(1)
    own.slope(gates[:2])
    nxt.slope(gates[2:])

    own.gather()
    nxt.gather()
    nxt.gather()
    own.gather(nxt.held[1])
    nxt.gather()
    own.gather()
    nxt_early = nxt.product(False, own.held[2])
    nxt_came_early = along_depth(nxt_early[2].astype(bf16), 2).astype(f32)
    nxt.gather()
    own.gather()
    own_early = own.product(False, own.held[3])

    def shared(result):
        share = result.shape[0] // COLS
        result = result.astype(bf16)

        def piece_of(y):
            return lax.dynamic_slice_in_dim(result, y % COLS * share, share, 0)

        return [piece_of(col)] + [along_y(piece_of(col + i), i) for i in range(1, COLS)]

    pieces_early = shared(own_early[2] + nxt_came_early)
    nxt_late = nxt.product(True)
    nxt_came_late = along_depth(nxt_late[2].astype(bf16), 2).astype(f32)
    own_late = own.product(True)
    pieces_late = shared(own_late[2] + nxt_came_late)

    parts = (nxt_early, nxt_late, own_early, own_late)
    x_all = jnp.concatenate([p[0] for p in parts])
    grads = jnp.concatenate([p[1] for p in parts])
    theirs = matmul(x_all, grads[:, hidden:], ((0,), (0,))).astype(bf16)
    theirs = other_core(theirs).astype(f32)
    grad_weight = (matmul(x_all, grads[:, :hidden], ((0,), (0,))) + theirs).astype(bf16)

    sides = []
    for pieces in (pieces_early, pieces_late):
        total = sum(p.astype(f32) for p in pieces).astype(bf16)
        mine = jnp.stack([total[:part], other_core(total[part:])])
        around = jnp.stack([mine] + [along_y(mine, -i) for i in range(1, COLS)])
        around = rolled(around, (COLS - col) % COLS)
        sides.append(around)
    (one_f, one_s, two_f, two_s), (nil_f, three_f, three_s, four_f) = sides

    def side(x, c):
        return jnp.where(core == c, x[0], x[1])

    pairs = [(side(nil_f, 0), side(nil_f, 1))]
    pairs += [(side(f, 0), side(s, 0)) for f, s in ((one_f, one_s), (two_f, two_s), (three_f, three_s))]
    pairs += [(side(four_f, 0), side(four_f, 1))]
    pairs += [(side(s, 1), side(f, 1)) for f, s in ((three_f, three_s), (two_f, two_s), (one_f, one_s))]
    result = jnp.stack([jnp.stack(p) for p in pairs])
    result = rolled(result, (RING - z) % RING)
    result = jnp.where(half == 0, result, result[:, ::-1])
    return (result.reshape(tokens, width), grad_weight)


def solution(mesh):
    placed = (P("depth", "row"), P("row", "col"), P("depth", ("col", "row")))
    return jax.shard_map(
        body,
        mesh=mesh,
        in_specs=placed,
        out_specs=(P("depth", "row"), P("row", ("col", "depth"))),
        check_vma=False,
    )
```

```python
import math

import jax
import jax.numpy as jnp
from jax import lax
from jax.sharding import PartitionSpec as P

GELU_FACTOR = math.sqrt(2.0 / math.pi)
GELU_CUBIC = 0.044715

ROWS, COLS, DEPTHS = 16, 4, 4
RING = 8
AXES = ("row", "col", "depth")


def gelu_slope(values):
    argument = GELU_FACTOR * (values + GELU_CUBIC * values * values * values)
    tangent = jnp.tanh(argument)
    return 0.5 * (1.0 + tangent) + 0.5 * values * (1.0 - tangent * tangent) * GELU_FACTOR * (
        1.0 + 3.0 * GELU_CUBIC * values * values
    )


def send(x, target):
    perm = []
    for r in range(ROWS):
        for c in range(COLS):
            for d in range(DEPTHS):
                tz, th, tc, td = target(r // 2, r % 2, c, d)
                dst = (((tz % RING) * 2 + th) * COLS + tc % COLS) * DEPTHS + td
                perm.append(((r * COLS + c) * DEPTHS + d, dst))
    return lax.ppermute(x, AXES, perm)


def along_ring(x, back=False):
    return send(x, lambda z, h, y, d: (z + (1 if d % 2 == int(back) else -1), h, y, d))


def other_half(x):
    return send(x, lambda z, h, y, d: (z, 1 - h, y, d))


def along_y(x, step):
    return send(x, lambda z, h, y, d: (z, h, y + step, d))


def along_depth(x, mask):
    return send(x, lambda z, h, y, d: (z, h, y, d ^ mask))


def other_core(x):
    return along_depth(x, 1)


def rolled(x, shift):
    n = x.shape[0]
    return lax.dynamic_slice_in_dim(jnp.concatenate([x, x]), shift, n, 0)


def matmul(a, b, dims):
    return lax.dot_general(a, b, (dims, ((), ())), preferred_element_type=jnp.float32)


def after(x, *others):
    return lax.optimization_barrier((x, *others))[0]


def body(inputs, up_weight, grad_hidden):
    row, col, depth = (lax.axis_index(name) for name in AXES)
    z, half, core = row // 2, row % 2, depth % 2
    tokens, width = inputs.shape
    part = tokens // ROWS
    slot = 2 * part
    hidden = up_weight.shape[1] // DEPTHS
    f32, bf16 = jnp.float32, jnp.bfloat16

    def swapped(x):
        return jnp.concatenate([x[i * part : (i + 1) * part] for i in (3, 2, 1, 0)])

    x = inputs.reshape(RING, 2, part, width)
    x = rolled(jnp.where(half == 0, x, x[:, ::-1]), z)
    x_up = x[:5]
    x_down = jnp.stack([x[-j % RING, ::-1] for j in range(5)])
    x_mine = jnp.where(core == 0, x_up, x_down)
    x_other = jnp.where(core == 0, x_down, x_up)
    x_core = other_core(x_other)
    x_next, x_far = [
        [along_depth(x[piece], mask) for piece in (slice(3, 5), slice(0, 3))]
        for x, mask in ((x_mine, 2), (x_other, 3))
    ]

    weight = lax.dynamic_slice_in_dim(up_weight, depth // 2 * 2 * hidden, 2 * hidden, 1)
    weight = lax.optimization_barrier(weight)

    def quarter(x, c):
        return lax.dynamic_slice_in_dim(x, c * hidden, hidden, 1)

    class Stream:
        def __init__(self):
            self.x = [None] * 5

        def tokens(self, slots, first, second):
            x = jnp.stack([first, second], axis=2)
            for i, j in enumerate(slots):
                self.x[j] = x[i].reshape(2 * slot, width)

        def scatter(self, j):
            if j == 4:
                sent = matmul(self.x[4][:slot], weight, ((1,), (0,))).astype(bf16)
                self.came = along_ring(sent)
            else:
                came = self.came.astype(f32)
                if j == 3:
                    came = jnp.concatenate([came, jnp.zeros_like(came)])
                sent = (matmul(self.x[j], weight, ((1,), (0,))) + came).astype(bf16)
                self.came = along_ring(sent)
            return sent

        def exchange(self):
            self.swap = other_core(swapped(quarter(self.came, 1 - core)))

        def slope(self, gates):
            total = matmul(self.x[0], quarter(weight, core), ((1,), (0,)))
            total = total + quarter(self.came, core).astype(f32) + self.swap.astype(f32)
            total = total[:slot] + other_half(total[slot:].astype(bf16)).astype(f32)
            gate = jnp.concatenate(gates)
            grad = (gate.astype(f32) * gelu_slope(total)).astype(bf16)
            both = jnp.concatenate([grad, other_half(grad)])
            others = swapped(other_core(both))
            self.held = [
                jnp.where(
                    core == 0,
                    jnp.concatenate([both, others], axis=1),
                    jnp.concatenate([others, both], axis=1),
                )
            ]

        def gather(self):
            ahead = self.held[-1]
            if len(self.held) == 4:
                ahead = ahead[:slot]
            self.held.append(along_ring(ahead, back=True))

        def product(self, slots, *others):
            held = [self.held[j][:slot] if j in (0, 4) else self.held[j] for j in slots]
            x = [self.x[j][:slot] if j in (0, 4) else self.x[j] for j in slots]
            grads = jnp.concatenate([after(held[0], *others)] + held[1:])
            result = matmul(grads, weight, ((1,), (1,)))
            return jnp.concatenate(x), grads, result

    own, nxt = Stream(), Stream()
    own.tokens(range(5), x_mine, x_core)
    own.scatter(4)
    nxt.tokens((3, 4), after(x_next[0], own.came), after(x_far[0], own.came))
    nxt.scatter(4)
    own.scatter(3)
    nxt.tokens((0, 1, 2), after(x_next[1], own.came), after(x_far[1], own.came))

    grad_hidden = after(grad_hidden, own.scatter(2)).reshape(RING, 2, part, hidden // 4)
    grad_hidden = jnp.where(z // 2 % 2 == 0, grad_hidden, grad_hidden[:, ::-1])
    grad_hidden = grad_hidden.reshape(ROWS, part, hidden // 4)
    came = lax.all_to_all(grad_hidden, "row", 0, 0)
    own.scatter(1)
    own.exchange()
    came = after(came.reshape(4, 4, part, hidden // 4), own.swap)
    gates = []
    for m in range(DEPTHS):
        gate = lax.dynamic_index_in_dim(came, depth ^ m, 0, keepdims=False)
        gate = along_depth(gate, m) if m else gate
        gates.append(gate.transpose(1, 0, 2).reshape(part, hidden))
    for j in (3, 2, 1):
        nxt.scatter(j)
    nxt.exchange()
    own.slope(gates[:2])
    nxt.slope(gates[2:])
    for j in range(4):
        own.gather()
        nxt.gather()

    def shared(result):
        share = result.shape[0] // COLS
        result = result.astype(bf16)

        def piece_of(y):
            return lax.dynamic_slice_in_dim(result, y % COLS * share, share, 0)

        return [piece_of(col)] + [along_y(piece_of(col + i), i) for i in range(1, COLS)]

    def to_owner(result):
        return along_depth(result.astype(bf16), 2).astype(f32)

    two, three, four = ((own.held[j], nxt.held[j]) for j in (2, 3, 4))
    parts = [nxt.product((1, 2), *two), own.product((1, 2), *three)]
    early = to_owner(parts[0][2])
    parts += [nxt.product((0, 3), *three)]
    late = [to_owner(parts[2][2])]
    parts += [nxt.product((4,), four[1]), own.product((0, 3, 4), *four)]
    late += [to_owner(parts[3][2])]
    pieces_early = shared(parts[1][2] + early)
    pieces_late = shared(parts[4][2] + jnp.concatenate(late))

    x_all = jnp.concatenate([p[0] for p in parts])
    grads = after(jnp.concatenate([p[1] for p in parts]), parts[4][2])
    theirs = matmul(x_all, quarter(grads, 1 - core), ((0,), (0,))).astype(bf16)
    theirs = other_core(theirs).astype(f32)
    grad_weight = (matmul(x_all, quarter(grads, core), ((0,), (0,))) + theirs).astype(bf16)

    pieces_early[0] = after(pieces_early[0], parts[4][2])
    sides = []
    for pieces in (pieces_early, pieces_late):
        total = sum(p.astype(f32) for p in pieces).astype(bf16)
        mine = jnp.stack([total[:part], other_core(total[part:])])
        around = jnp.stack([mine] + [along_y(mine, -i) for i in range(1, COLS)])
        around = rolled(around, (COLS - col) % COLS)
        sides.append(around)
    (one_f, one_s, two_f, two_s), (nil_f, three_f, three_s, four_f) = sides

    def side(x, c):
        return jnp.where(core == c, x[0], x[1])

    pairs = [(side(nil_f, 0), side(nil_f, 1))]
    pairs += [(side(f, 0), side(s, 0)) for f, s in ((one_f, one_s), (two_f, two_s), (three_f, three_s))]
    pairs += [(side(four_f, 0), side(four_f, 1))]
    pairs += [(side(s, 1), side(f, 1)) for f, s in ((three_f, three_s), (two_f, two_s), (one_f, one_s))]
    result = jnp.stack([jnp.stack(p) for p in pairs])
    result = rolled(result, (RING - z) % RING)
    result = jnp.where(half == 0, result, result[:, ::-1])
    return (result.reshape(tokens, width), grad_weight)


def solution(mesh):
    placed = (P("depth", "row"), P("row", "col"), P("depth", ("col", "row")))
    return jax.shard_map(
        body,
        mesh=mesh,
        in_specs=placed,
        out_specs=(P("depth", "row"), P("row", ("col", "depth"))),
        check_vma=False,
    )
```

```python
import math

import jax
import jax.numpy as jnp
from jax import lax
from jax.sharding import PartitionSpec as P

GELU_FACTOR = math.sqrt(2.0 / math.pi)
GELU_CUBIC = 0.044715

ROWS, COLS, DEPTHS = 16, 4, 4
RING = 8
AXES = ("row", "col", "depth")


def gelu_slope(values):
    argument = GELU_FACTOR * (values + GELU_CUBIC * values * values * values)
    tangent = jnp.tanh(argument)
    return 0.5 * (1.0 + tangent) + 0.5 * values * (1.0 - tangent * tangent) * GELU_FACTOR * (
        1.0 + 3.0 * GELU_CUBIC * values * values
    )


def send(x, target):
    perm = []
    for r in range(ROWS):
        for c in range(COLS):
            for d in range(DEPTHS):
                tz, th, tc, td = target(r // 2, r % 2, c, d)
                dst = (((tz % RING) * 2 + th) * COLS + tc % COLS) * DEPTHS + td
                perm.append(((r * COLS + c) * DEPTHS + d, dst))
    return lax.ppermute(x, AXES, perm)


def along_ring(x, back=False):
    return send(x, lambda z, h, y, d: (z + (1 if d % 2 == int(back) else -1), h, y, d))


def other_half(x):
    return send(x, lambda z, h, y, d: (z, 1 - h, y, d))


def along_y(x, step):
    return send(x, lambda z, h, y, d: (z, h, y + step, d))


def along_depth(x, mask):
    return send(x, lambda z, h, y, d: (z, h, y, d ^ mask))


def other_core(x):
    return along_depth(x, 1)


def rolled(x, shift):
    n = x.shape[0]
    return lax.dynamic_slice_in_dim(jnp.concatenate([x, x]), shift, n, 0)


def matmul(a, b, dims):
    return lax.dot_general(a, b, (dims, ((), ())), preferred_element_type=jnp.float32)


def after(x, *others):
    return lax.optimization_barrier((x, *others))[0]


def body(inputs, up_weight, grad_hidden):
    row, col, depth = (lax.axis_index(name) for name in AXES)
    z, half, core = row // 2, row % 2, depth % 2
    tokens, width = inputs.shape
    part = tokens // ROWS
    slot = 2 * part
    hidden = up_weight.shape[1] // DEPTHS
    f32, bf16 = jnp.float32, jnp.bfloat16

    def swapped(x):
        return jnp.concatenate([x[i * part : (i + 1) * part] for i in (3, 2, 1, 0)])

    x = inputs.reshape(RING, 2, part, width)
    x = rolled(jnp.where(half == 0, x, x[:, ::-1]), z)
    x_up = x[:5]
    x_down = jnp.stack([x[-j % RING, ::-1] for j in range(5)])
    x_mine = jnp.where(core == 0, x_up, x_down)
    x_other = jnp.where(core == 0, x_down, x_up)
    x_core = other_core(x_other)
    x_next, x_far = [
        [along_depth(x[piece], mask) for piece in (slice(3, 5), slice(0, 3))]
        for x, mask in ((x_mine, 2), (x_other, 3))
    ]

    weight = lax.dynamic_slice_in_dim(up_weight, depth // 2 * 2 * hidden, 2 * hidden, 1)
    weight = lax.optimization_barrier(weight)

    def quarter(x, c):
        return lax.dynamic_slice_in_dim(x, c * hidden, hidden, 1)

    class Stream:
        def __init__(self):
            self.x = [None] * 5

        def tokens(self, slots, first, second):
            x = jnp.stack([first, second], axis=2)
            for i, j in enumerate(slots):
                self.x[j] = x[i].reshape(2 * slot, width)

        def scatter(self, j):
            if j == 4:
                sent = matmul(self.x[4][:slot], weight, ((1,), (0,))).astype(bf16)
                self.came = along_ring(sent)
            else:
                came = self.came.astype(f32)
                if j == 3:
                    came = jnp.concatenate([came, jnp.zeros_like(came)])
                sent = (matmul(self.x[j], weight, ((1,), (0,))) + came).astype(bf16)
                self.came = along_ring(sent)
            return sent

        def exchange(self):
            self.swap = other_core(swapped(quarter(self.came, 1 - core)))

        def slope(self, gate):
            total = matmul(self.x[0], quarter(weight, core), ((1,), (0,)))
            total = total + quarter(self.came, core).astype(f32) + self.swap.astype(f32)
            sent = total.astype(bf16)
            sent = jnp.concatenate([sent[slot:], sent[:slot]])
            total = total + other_half(sent).astype(f32)
            self.grad = (gate.astype(f32) * gelu_slope(total)).astype(bf16)

        def begin(self):
            others = swapped(other_core(self.grad))
            self.held = [
                jnp.where(
                    core == 0,
                    jnp.concatenate([self.grad, others], axis=1),
                    jnp.concatenate([others, self.grad], axis=1),
                )
            ]

        def gather(self):
            ahead = self.held[-1]
            if len(self.held) == 4:
                ahead = ahead[:slot]
            self.held.append(along_ring(ahead, back=True))

        def product(self, slots, *others):
            held = [self.held[j][:slot] if j in (0, 4) else self.held[j] for j in slots]
            x = [self.x[j][:slot] if j in (0, 4) else self.x[j] for j in slots]
            grads = jnp.concatenate([after(held[0], *others)] + held[1:])
            result = matmul(grads, weight, ((1,), (1,)))
            return jnp.concatenate(x), grads, result

    own, nxt = Stream(), Stream()
    own.tokens(range(5), x_mine, after(x_core, x_next[0], x_far[0]))
    own.scatter(4)
    nxt.tokens((3, 4), x_next[0], x_far[0])
    nxt.scatter(4)
    own.scatter(3)
    nxt.tokens((0, 1, 2), after(x_next[1], own.came), after(x_far[1], own.came))

    gate = after(grad_hidden, own.scatter(2)).reshape(RING, 2, part, hidden // 4)
    gate = (gate, gate[:, ::-1])
    gate = [jnp.where(z // 2 % 2 == h, *gate) for h in range(2)]
    gate = jnp.stack(gate, axis=1).reshape(ROWS, slot, hidden // 4)
    came = lax.all_to_all(gate, "row", 0, 0)
    own.scatter(1)
    own.exchange()
    came = after(came.reshape(4, 4, slot, hidden // 4), own.swap)
    gates = []
    for m in range(DEPTHS):
        gate = lax.dynamic_index_in_dim(came, depth ^ m, 0, keepdims=False)
        gate = along_depth(gate, m) if m else gate
        gates.append(gate.reshape(4, 2, part, hidden // 4))
    for j in (3, 2, 1):
        nxt.scatter(j)
    nxt.exchange()
    for s, stream in enumerate((own, nxt)):
        gate = jnp.stack(gates[2 * s : 2 * s + 2])
        stream.slope(gate.transpose(2, 0, 3, 1, 4).reshape(2 * slot, hidden))
    nxt.begin()
    own.begin()
    own.held[0] = after(own.held[0], nxt.held[0])
    for j in range(4):
        nxt.gather()
        own.gather()

    def shared(result):
        share = result.shape[0] // COLS
        result = result.astype(bf16)

        def piece_of(y):
            return lax.dynamic_slice_in_dim(result, y % COLS * share, share, 0)

        return [piece_of(col)] + [along_y(piece_of(col + i), i) for i in range(1, COLS)]

    def to_owner(result):
        return along_depth(result.astype(bf16), 2).astype(f32)

    two, three = ((own.held[j], nxt.held[j]) for j in (2, 3))
    parts = [nxt.product((0, 1, 2), *two)]
    early = to_owner(parts[0][2])
    parts += [own.product((1, 2), *three)]
    parts += [nxt.product((3, 4))]
    late = to_owner(parts[2][2])
    parts += [own.product((0, 3, 4))]
    pieces_early = shared(parts[1][2] + early[slot:])
    pieces_early[0] = after(pieces_early[0], own.held[4])
    pieces_late = shared(parts[3][2] + jnp.concatenate([early[:slot], late]))

    x_all = jnp.concatenate([p[0] for p in parts])
    grads = after(jnp.concatenate([p[1] for p in parts]), parts[3][2])
    theirs = matmul(x_all, quarter(grads, 1 - core), ((0,), (0,))).astype(bf16)
    theirs = other_core(theirs).astype(f32)
    grad_weight = (matmul(x_all, quarter(grads, core), ((0,), (0,))) + theirs).astype(bf16)

    total = [sum(p.astype(f32) for p in pieces).astype(bf16) for pieces in (pieces_early, pieces_late)]
    mine = jnp.stack([t[:part] for t in total])
    theirs = other_core(jnp.stack([t[part:] for t in total]))
    mine = jnp.stack([mine, theirs], axis=1)
    around = jnp.stack([mine] + [along_y(mine, -i) for i in range(1, COLS)])
    around = after(around, grad_weight)
    around = rolled(around, (COLS - col) % COLS)
    sides = [[around[y, n] for y in range(COLS)] for n in range(2)]
    (one_f, one_s, two_f, two_s), (nil_f, three_f, three_s, four_f) = sides

    def side(x, c):
        return jnp.where(core == c, x[0], x[1])

    pairs = [(side(nil_f, 0), side(nil_f, 1))]
    pairs += [(side(f, 0), side(s, 0)) for f, s in ((one_f, one_s), (two_f, two_s), (three_f, three_s))]
    pairs += [(side(four_f, 0), side(four_f, 1))]
    pairs += [(side(s, 1), side(f, 1)) for f, s in ((three_f, three_s), (two_f, two_s), (one_f, one_s))]
    result = jnp.stack([jnp.stack(p) for p in pairs])
    result = rolled(result, (RING - z) % RING)
    result = jnp.where(half == 0, result, result[:, ::-1])
    return (result.reshape(tokens, width), grad_weight)


def solution(mesh):
    placed = (P("depth", "row"), P("row", "col"), P("depth", ("col", "row")))
    return jax.shard_map(
        body,
        mesh=mesh,
        in_specs=placed,
        out_specs=(P("depth", "row"), P("row", ("col", "depth"))),
        check_vma=False,
    )
```

```python
import math

import jax
import jax.numpy as jnp
from jax import lax
from jax.sharding import PartitionSpec as P

GELU_FACTOR = math.sqrt(2.0 / math.pi)
GELU_CUBIC = 0.044715

ROWS, COLS, DEPTHS = 16, 4, 4
RING = 8
AXES = ("row", "col", "depth")


def gelu_slope(values):
    argument = GELU_FACTOR * (values + GELU_CUBIC * values * values * values)
    tangent = jnp.tanh(argument)
    return 0.5 * (1.0 + tangent) + 0.5 * values * (1.0 - tangent * tangent) * GELU_FACTOR * (
        1.0 + 3.0 * GELU_CUBIC * values * values
    )


def send(x, target):
    perm = []
    for r in range(ROWS):
        for c in range(COLS):
            for d in range(DEPTHS):
                tz, th, tc, td = target(r // 2, r % 2, c, d)
                dst = (((tz % RING) * 2 + th) * COLS + tc % COLS) * DEPTHS + td
                perm.append(((r * COLS + c) * DEPTHS + d, dst))
    return lax.ppermute(x, AXES, perm)


def along_ring(x, back=False):
    return send(x, lambda z, h, y, d: (z + (1 if d % 2 == int(back) else -1), h, y, d))


def other_half(x):
    return send(x, lambda z, h, y, d: (z, 1 - h, y, d))


def along_y(x, step):
    return send(x, lambda z, h, y, d: (z, h, y + step, d))


def along_depth(x, mask):
    return send(x, lambda z, h, y, d: (z, h, y, d ^ mask))


def other_core(x):
    return along_depth(x, 1)


def rolled(x, shift):
    n = x.shape[0]
    return lax.dynamic_slice_in_dim(jnp.concatenate([x, x]), shift, n, 0)


def matmul(a, b, dims):
    return lax.dot_general(a, b, (dims, ((), ())), preferred_element_type=jnp.float32)


def after(x, *others):
    return lax.optimization_barrier((x, *others))[0]


def body(inputs, up_weight, grad_hidden):
    row, col, depth = (lax.axis_index(name) for name in AXES)
    z, half, core = row // 2, row % 2, depth % 2
    tokens, width = inputs.shape
    part = tokens // ROWS
    slot = 2 * part
    hidden = up_weight.shape[1] // DEPTHS
    f32, bf16 = jnp.float32, jnp.bfloat16

    def swapped(x):
        return jnp.concatenate([x[i * part : (i + 1) * part] for i in (3, 2, 1, 0)])

    x = inputs.reshape(RING, 2, part, width)
    x = rolled(jnp.where(half == 0, x, x[:, ::-1]), z)
    x_up = x[:5]
    x_down = jnp.stack([x[-j % RING, ::-1] for j in range(5)])
    x_mine = jnp.where(core == 0, x_up, x_down)
    x_other = jnp.where(core == 0, x_down, x_up)
    x_core = other_core(x_other)
    x_next, x_far = [
        [along_depth(x[piece], mask) for piece in (slice(3, 5), slice(0, 3))]
        for x, mask in ((x_mine, 2), (x_other, 3))
    ]

    weight = lax.dynamic_slice_in_dim(up_weight, depth // 2 * 2 * hidden, 2 * hidden, 1)
    weight = lax.optimization_barrier(weight)

    def quarter(x, c):
        return lax.dynamic_slice_in_dim(x, c * hidden, hidden, 1)

    class Stream:
        def __init__(self):
            self.x = [None] * 5

        def tokens(self, slots, first, second):
            x = jnp.stack([first, second], axis=2)
            for i, j in enumerate(slots):
                self.x[j] = x[i].reshape(2 * slot, width)

        def scatter(self, j, *others):
            if j == 4:
                sent = matmul(self.x[4][:slot], weight, ((1,), (0,))).astype(bf16)
                self.came = along_ring(sent)
            else:
                came = self.came.astype(f32)
                if j == 3:
                    came = jnp.concatenate([came, jnp.zeros_like(came)])
                x = after(self.x[j], *others) if others else self.x[j]
                sent = (matmul(x, weight, ((1,), (0,))) + came).astype(bf16)
                self.came = along_ring(sent)
            return sent

        def exchange(self):
            self.swap = other_core(swapped(quarter(self.came, 1 - core)))

        def at_home(self):
            home = matmul(self.x[0], quarter(weight, core), ((1,), (0,)))
            self.home = lax.optimization_barrier(home)
            return self.home

        def slope(self, gates, *others):
            total = self.home + quarter(self.came, core).astype(f32) + self.swap.astype(f32)
            total = total[:slot] + other_half(total[slot:].astype(bf16)).astype(f32)
            gate = jnp.concatenate(gates)
            grad = (gate.astype(f32) * gelu_slope(total)).astype(bf16)
            both = jnp.concatenate([grad, other_half(grad)])
            theirs = other_core(both)
            if others:
                theirs = after(theirs, *others)
            others = swapped(theirs)
            self.held = [
                jnp.where(
                    core == 0,
                    jnp.concatenate([both, others], axis=1),
                    jnp.concatenate([others, both], axis=1),
                )
            ]

        def gather(self):
            ahead = self.held[-1]
            if len(self.held) == 4:
                ahead = ahead[:slot]
            self.held.append(along_ring(ahead, back=True))

        def product(self, slots, *others):
            held = [self.held[j][:slot] if j in (0, 4) else self.held[j] for j in slots]
            x = [self.x[j][:slot] if j in (0, 4) else self.x[j] for j in slots]
            grads = jnp.concatenate([after(held[0], *others)] + held[1:])
            result = matmul(grads, weight, ((1,), (1,)))
            return jnp.concatenate(x), grads, result

    own, nxt = Stream(), Stream()
    own.tokens(range(5), x_mine, after(x_core, x_next[0], x_far[0]))
    own.scatter(4)
    nxt.tokens((3, 4), x_next[0], x_far[0])
    nxt.scatter(4)
    own.scatter(3)
    nxt.tokens((0, 1, 2), after(x_next[1], own.came), after(x_far[1], own.came))

    own.scatter(2)
    nxt.scatter(3)

    grad_hidden = after(grad_hidden, nxt.scatter(2)).reshape(RING, 2, part, hidden // 4)
    grad_hidden = jnp.where(z // 2 % 2 == 0, grad_hidden, grad_hidden[:, ::-1])
    grad_hidden = grad_hidden.reshape(ROWS, part, hidden // 4)
    came = lax.all_to_all(grad_hidden, "row", 0, 0)
    own.scatter(1)
    came = after(came.reshape(4, 4, part, hidden // 4), nxt.came)
    gates = []
    for m in range(DEPTHS):
        gate = lax.dynamic_index_in_dim(came, depth ^ m, 0, keepdims=False)
        gate = along_depth(gate, m) if m else gate
        gates.append(gate.transpose(1, 0, 2).reshape(part, hidden))
    nxt.scatter(1, own.at_home(), nxt.at_home())
    own.exchange()
    nxt.exchange()
    nxt.slope(gates[2:])
    own.slope(gates[:2], nxt.held[0])
    for j in range(4):
        nxt.gather()
        own.gather()

    def to_owner(result):
        return along_depth(result.astype(bf16), 2).astype(f32)

    parts = [nxt.product((0, 1, 2), nxt.held[3])]
    early = to_owner(parts[0][2])
    parts += [own.product((1, 2), own.held[3])]
    result = [(parts[1][2] + early[slot:]).astype(bf16)]
    parts += [nxt.product((3, 4))]
    late = to_owner(parts[2][2])
    parts += [own.product((0, 3, 4))]
    result += [(parts[3][2] + jnp.concatenate([early[:slot], late])).astype(bf16)]

    result = jnp.stack(result).reshape(2, COLS, slot, width)
    pieces = [
        lax.dynamic_index_in_dim(result, (col + i) % COLS, 1, keepdims=False) for i in range(COLS)
    ]
    came = [pieces[0]] + [along_y(pieces[i], i) for i in range(1, COLS)]
    total = sum(c.astype(f32) for c in came).astype(bf16)

    x_all = jnp.concatenate([p[0] for p in parts])
    grads = after(jnp.concatenate([p[1] for p in parts]), *pieces[1:])
    theirs = matmul(x_all, quarter(grads, 1 - core), ((0,), (0,))).astype(bf16)
    theirs = other_core(theirs).astype(f32)

    mine = jnp.stack([total[:, :part], other_core(total[:, part:])], axis=1)
    around = jnp.stack([mine] + [along_y(mine, -i) for i in range(1, COLS)])
    x_all = after(x_all, mine)
    grad_weight = (matmul(x_all, quarter(grads, core), ((0,), (0,))) + theirs).astype(bf16)
    around = rolled(around, (COLS - col) % COLS)
    sides = [[around[y, n] for y in range(COLS)] for n in range(2)]
    (one_f, one_s, two_f, two_s), (nil_f, three_f, three_s, four_f) = sides

    def side(x, c):
        return jnp.where(core == c, x[0], x[1])

    pairs = [(side(nil_f, 0), side(nil_f, 1))]
    pairs += [(side(f, 0), side(s, 0)) for f, s in ((one_f, one_s), (two_f, two_s), (three_f, three_s))]
    pairs += [(side(four_f, 0), side(four_f, 1))]
    pairs += [(side(s, 1), side(f, 1)) for f, s in ((three_f, three_s), (two_f, two_s), (one_f, one_s))]
    result = jnp.stack([jnp.stack(p) for p in pairs])
    result = rolled(result, (RING - z) % RING)
    result = jnp.where(half == 0, result, result[:, ::-1])
    return (result.reshape(tokens, width), grad_weight)


def solution(mesh):
    placed = (P("depth", "row"), P("row", "col"), P("depth", ("col", "row")))
    return jax.shard_map(
        body,
        mesh=mesh,
        in_specs=placed,
        out_specs=(P("depth", "row"), P("row", ("col", "depth"))),
        check_vma=False,
    )
```

```python
import math

import jax
import jax.numpy as jnp
from jax import lax
from jax.sharding import PartitionSpec as P

GELU_FACTOR = math.sqrt(2.0 / math.pi)
GELU_CUBIC = 0.044715

ROWS, COLS, DEPTHS = 16, 4, 4
RING = 8
AXES = ("row", "col", "depth")


def gelu_slope(values):
    argument = GELU_FACTOR * (values + GELU_CUBIC * values * values * values)
    tangent = jnp.tanh(argument)
    return 0.5 * (1.0 + tangent) + 0.5 * values * (1.0 - tangent * tangent) * GELU_FACTOR * (
        1.0 + 3.0 * GELU_CUBIC * values * values
    )


def send(x, target):
    perm = []
    for r in range(ROWS):
        for c in range(COLS):
            for d in range(DEPTHS):
                tz, th, tc, td = target(r // 2, r % 2, c, d)
                dst = (((tz % RING) * 2 + th) * COLS + tc % COLS) * DEPTHS + td
                perm.append(((r * COLS + c) * DEPTHS + d, dst))
    return lax.ppermute(x, AXES, perm)


def along_ring(x, back=False):
    return send(x, lambda z, h, y, d: (z + (1 if d % 2 == int(back) else -1), h, y, d))


def other_half(x):
    return send(x, lambda z, h, y, d: (z, 1 - h, y, d))


def along_y(x, step):
    return send(x, lambda z, h, y, d: (z, h, y + step, d))


def along_depth(x, mask):
    return send(x, lambda z, h, y, d: (z, h, y, d ^ mask))


def other_core(x):
    return along_depth(x, 1)


def rolled(x, shift):
    n = x.shape[0]
    return lax.dynamic_slice_in_dim(jnp.concatenate([x, x]), shift, n, 0)


def matmul(a, b, dims):
    return lax.dot_general(a, b, (dims, ((), ())), preferred_element_type=jnp.float32)


def after(x, *others):
    return lax.optimization_barrier((x, *others))[0]


def body(inputs, up_weight, grad_hidden):
    row, col, depth = (lax.axis_index(name) for name in AXES)
    z, half, core = row // 2, row % 2, depth % 2
    tokens, width = inputs.shape
    part = tokens // ROWS
    slot = 2 * part
    hidden = up_weight.shape[1] // DEPTHS
    f32, bf16 = jnp.float32, jnp.bfloat16

    def swapped(x):
        return jnp.concatenate([x[i * part : (i + 1) * part] for i in (3, 2, 1, 0)])

    x = inputs.reshape(RING, 2, part, width)
    x = rolled(jnp.where(half == 0, x, x[:, ::-1]), z)
    x_up = x[:5]
    x_down = jnp.stack([x[-j % RING, ::-1] for j in range(5)])
    x_mine = jnp.where(core == 0, x_up, x_down)
    x_other = jnp.where(core == 0, x_down, x_up)
    x_core = other_core(x_other)
    x_next, x_far = [
        [along_depth(x[piece], mask) for piece in (slice(3, 5), slice(0, 3))]
        for x, mask in ((x_mine, 2), (x_other, 3))
    ]

    weight = lax.dynamic_slice_in_dim(up_weight, depth // 2 * 2 * hidden, 2 * hidden, 1)
    weight = lax.optimization_barrier(weight)

    def quarter(x, c):
        return lax.dynamic_slice_in_dim(x, c * hidden, hidden, 1)

    class Stream:
        def __init__(self):
            self.x = [None] * 5

        def tokens(self, slots, first, second):
            x = jnp.stack([first, second], axis=2)
            for i, j in enumerate(slots):
                self.x[j] = x[i].reshape(2 * slot, width)

        def scatter(self, j, *others):
            if j == 4:
                sent = matmul(self.x[4][:slot], weight, ((1,), (0,))).astype(bf16)
                self.came = along_ring(sent)
            else:
                came = self.came.astype(f32)
                if j == 3:
                    came = jnp.concatenate([came, jnp.zeros_like(came)])
                x = after(self.x[j], *others) if others else self.x[j]
                sent = (matmul(x, weight, ((1,), (0,))) + came).astype(bf16)
                self.came = along_ring(sent)
            return sent

        def exchange(self):
            self.swap = other_core(swapped(quarter(self.came, 1 - core)))

        def at_home(self):
            home = matmul(self.x[0], quarter(weight, core), ((1,), (0,)))
            self.home = lax.optimization_barrier(home)
            return self.home

        def slope(self, gates, *others):
            total = self.home + quarter(self.came, core).astype(f32) + self.swap.astype(f32)
            total = total[:slot] + other_half(total[slot:].astype(bf16)).astype(f32)
            gates = [after(g, self.swap) for g in gates]
            gate = jnp.concatenate([g.transpose(1, 0, 2).reshape(part, hidden) for g in gates])
            grad = (gate.astype(f32) * gelu_slope(total)).astype(bf16)
            both = jnp.concatenate([grad, other_half(grad)])
            theirs = other_core(both)
            if others:
                theirs = after(theirs, *others)
            others = swapped(theirs)
            self.held = [
                jnp.where(
                    core == 0,
                    jnp.concatenate([both, others], axis=1),
                    jnp.concatenate([others, both], axis=1),
                )
            ]

        def gather(self):
            ahead = self.held[-1]
            if len(self.held) == 4:
                ahead = ahead[:slot]
            self.held.append(along_ring(ahead, back=True))

        def product(self, slots, *others):
            held = [self.held[j][:slot] if j in (0, 4) else self.held[j] for j in slots]
            x = [self.x[j][:slot] if j in (0, 4) else self.x[j] for j in slots]
            grads = jnp.concatenate([after(held[0], *others)] + held[1:])
            result = lax.optimization_barrier(matmul(grads, weight, ((1,), (1,))))
            return jnp.concatenate(x), grads, result

    own, nxt = Stream(), Stream()
    own.tokens(range(5), x_mine, after(x_core, x_next[0], x_far[0]))
    own.scatter(4)
    nxt.tokens((3, 4), x_next[0], x_far[0])
    nxt.scatter(4)
    own.scatter(3)
    nxt.tokens((0, 1, 2), after(x_next[1], own.came), after(x_far[1], own.came))

    own.scatter(2)
    nxt.scatter(3)

    grad_hidden = after(grad_hidden, nxt.scatter(2)).reshape(RING, 2, part, hidden // 4)
    grad_hidden = jnp.where(z // 2 % 2 == 0, grad_hidden, grad_hidden[:, ::-1])
    grad_hidden = grad_hidden.reshape(ROWS, part, hidden // 4)
    came = lax.all_to_all(grad_hidden, "row", 0, 0)
    own.scatter(1)
    came = after(came.reshape(4, 4, part, hidden // 4), nxt.came)
    gates = []
    for m in range(DEPTHS):
        gate = lax.dynamic_index_in_dim(came, depth ^ m, 0, keepdims=False)
        gate = along_depth(gate, m) if m else gate
        gates.append(gate)
    nxt.scatter(1, own.at_home(), nxt.at_home())
    own.exchange()
    nxt.exchange()
    nxt.slope(gates[2:])
    own.slope(gates[:2], nxt.held[0])
    for j in range(4):
        nxt.gather()
        own.gather()

    def to_owner(result):
        return along_depth(result.astype(bf16), 2).astype(f32)

    parts = [own.product((1, 2), nxt.held[2]), nxt.product((0, 1, 2), own.held[3])]
    back = [to_owner(parts[1][2])]
    parts += [nxt.product((3,)), own.product((0, 3), nxt.held[3])]
    back += [to_owner(parts[2][2])]
    parts += [nxt.product((4,)), own.product((4,))]
    back += [to_owner(parts[4][2])]
    result = [parts[0][2] + back[0][slot:]]
    result += [jnp.concatenate([parts[3][2], parts[5][2]])]
    result[1] = result[1] + jnp.concatenate([back[0][:slot]] + back[1:])
    result = [r.astype(bf16) for r in result]

    result = jnp.stack(result).reshape(2, COLS, slot, width)
    pieces = [
        lax.dynamic_index_in_dim(result, (col + i) % COLS, 1, keepdims=False) for i in range(COLS)
    ]
    came = [pieces[0]] + [along_y(pieces[i], i) for i in range(1, COLS)]

    x_all = jnp.concatenate([p[0] for p in parts])
    grads = after(jnp.concatenate([p[1] for p in parts]), *pieces[1:])
    theirs = matmul(x_all, quarter(grads, 1 - core), ((0,), (0,))).astype(bf16)
    came[0] = after(came[0], theirs)
    theirs = other_core(theirs).astype(f32)
    total = sum(c.astype(f32) for c in came).astype(bf16)

    mine = jnp.stack([total[:, :part], other_core(total[:, part:])], axis=1)
    around = jnp.stack([mine] + [along_y(mine, -i) for i in range(1, COLS)])
    x_all = after(x_all, mine)
    grad_weight = (matmul(x_all, quarter(grads, core), ((0,), (0,))) + theirs).astype(bf16)
    around = rolled(around, (COLS - col) % COLS)
    sides = [[around[y, n] for y in range(COLS)] for n in range(2)]
    (one_f, one_s, two_f, two_s), (nil_f, three_f, three_s, four_f) = sides

    def side(x, c):
        return jnp.where(core == c, x[0], x[1])

    pairs = [(side(nil_f, 0), side(nil_f, 1))]
    pairs += [(side(f, 0), side(s, 0)) for f, s in ((one_f, one_s), (two_f, two_s), (three_f, three_s))]
    pairs += [(side(four_f, 0), side(four_f, 1))]
    pairs += [(side(s, 1), side(f, 1)) for f, s in ((three_f, three_s), (two_f, two_s), (one_f, one_s))]
    result = jnp.stack([jnp.stack(p) for p in pairs])
    result = rolled(result, (RING - z) % RING)
    result = jnp.where(half == 0, result, result[:, ::-1])
    return (result.reshape(tokens, width), grad_weight)


def solution(mesh):
    placed = (P("depth", "row"), P("row", "col"), P("depth", ("col", "row")))
    return jax.shard_map(
        body,
        mesh=mesh,
        in_specs=placed,
        out_specs=(P("depth", "row"), P("row", ("col", "depth"))),
        check_vma=False,
    )
```

```python
import math

import jax
import jax.numpy as jnp
from jax import lax
from jax.sharding import PartitionSpec as P

GELU_FACTOR = math.sqrt(2.0 / math.pi)
GELU_CUBIC = 0.044715

ROWS, COLS, DEPTHS = 16, 4, 4
RING = 8
AXES = ("row", "col", "depth")


def gelu_slope(values):
    argument = GELU_FACTOR * (values + GELU_CUBIC * values * values * values)
    tangent = jnp.tanh(argument)
    return 0.5 * (1.0 + tangent) + 0.5 * values * (1.0 - tangent * tangent) * GELU_FACTOR * (
        1.0 + 3.0 * GELU_CUBIC * values * values
    )


def send(x, target):
    perm = []
    for r in range(ROWS):
        for c in range(COLS):
            for d in range(DEPTHS):
                tz, th, tc, td = target(r // 2, r % 2, c, d)
                dst = (((tz % RING) * 2 + th) * COLS + tc % COLS) * DEPTHS + td
                perm.append(((r * COLS + c) * DEPTHS + d, dst))
    return lax.ppermute(x, AXES, perm)


def along_ring(x, back=False):
    return send(x, lambda z, h, y, d: (z + (1 if d % 2 == int(back) else -1), h, y, d))


def other_half(x):
    return send(x, lambda z, h, y, d: (z, 1 - h, y, d))


def along_y(x, step):
    return send(x, lambda z, h, y, d: (z, h, y + step, d))


def along_depth(x, mask):
    return send(x, lambda z, h, y, d: (z, h, y, d ^ mask))


def other_core(x):
    return along_depth(x, 1)


def rolled(x, shift):
    n = x.shape[0]
    return lax.dynamic_slice_in_dim(jnp.concatenate([x, x]), shift, n, 0)


def matmul(a, b, dims):
    return lax.dot_general(a, b, (dims, ((), ())), preferred_element_type=jnp.float32)


def after(x, *others):
    return lax.optimization_barrier((x, *others))[0]


def body(inputs, up_weight, grad_hidden):
    row, col, depth = (lax.axis_index(name) for name in AXES)
    z, half, core = row // 2, row % 2, depth % 2
    tokens, width = inputs.shape
    part = tokens // ROWS
    slot = 2 * part
    hidden = up_weight.shape[1] // DEPTHS
    f32, bf16 = jnp.float32, jnp.bfloat16

    def swapped(x):
        return jnp.concatenate([x[i * part : (i + 1) * part] for i in (3, 2, 1, 0)])

    x = inputs.reshape(RING, 2, part, width)
    x = rolled(jnp.where(half == 0, x, x[:, ::-1]), z)
    x_up = x[:5]
    x_down = jnp.stack([x[-j % RING, ::-1] for j in range(5)])
    x_mine = jnp.where(core == 0, x_up, x_down)
    x_other = jnp.where(core == 0, x_down, x_up)
    x_core = other_core(x_other)
    x_next, x_far = [
        [along_depth(x[piece], mask) for piece in (slice(3, 5), slice(0, 3))]
        for x, mask in ((x_mine, 2), (x_other, 3))
    ]

    weight = lax.dynamic_slice_in_dim(up_weight, depth // 2 * 2 * hidden, 2 * hidden, 1)
    weight = lax.optimization_barrier(weight)

    def quarter(x, c):
        return lax.dynamic_slice_in_dim(x, c * hidden, hidden, 1)

    class Stream:
        def __init__(self):
            self.x = [None] * 5

        def tokens(self, slots, first, second):
            x = jnp.stack([first, second], axis=2)
            for i, j in enumerate(slots):
                self.x[j] = x[i].reshape(2 * slot, width)

        def scatter(self, j, *others):
            if j == 4:
                sent = matmul(self.x[4][:slot], weight, ((1,), (0,))).astype(bf16)
                self.came = along_ring(sent)
            else:
                came = self.came.astype(f32)
                if j == 3:
                    came = jnp.concatenate([came, jnp.zeros_like(came)])
                x = after(self.x[j], *others) if others else self.x[j]
                sent = (matmul(x, weight, ((1,), (0,))) + came).astype(bf16)
                self.came = along_ring(sent)
            return sent

        def exchange(self):
            self.swap = other_core(swapped(quarter(self.came, 1 - core)))

        def at_home(self):
            home = matmul(self.x[0], quarter(weight, core), ((1,), (0,)))
            self.home = lax.optimization_barrier(home)
            return self.home

        def slope(self, gates, *others):
            total = self.home + quarter(self.came, core).astype(f32) + self.swap.astype(f32)
            total = total[:slot] + other_half(total[slot:].astype(bf16)).astype(f32)
            gates = [after(g, self.swap) for g in gates]
            gate = jnp.concatenate([g.transpose(1, 0, 2).reshape(part, hidden) for g in gates])
            grad = (gate.astype(f32) * gelu_slope(total)).astype(bf16)
            both = jnp.concatenate([grad, other_half(grad)])
            theirs = other_core(both)
            if others:
                theirs = after(theirs, *others)
            others = swapped(theirs)
            self.held = [
                jnp.where(
                    core == 0,
                    jnp.concatenate([both, others], axis=1),
                    jnp.concatenate([others, both], axis=1),
                )
            ]

        def gather(self):
            ahead = self.held[-1]
            if len(self.held) == 4:
                ahead = ahead[:slot]
            self.held.append(along_ring(ahead, back=True))

        def product(self, slots, *others):
            held = [self.held[j][:slot] if j in (0, 4) else self.held[j] for j in slots]
            x = [self.x[j][:slot] if j in (0, 4) else self.x[j] for j in slots]
            grads = jnp.concatenate([after(held[0], *others)] + held[1:])
            result = lax.optimization_barrier(matmul(grads, weight, ((1,), (1,))))
            return jnp.concatenate(x), grads, result

    own, nxt = Stream(), Stream()
    own.tokens(range(5), x_mine, after(x_core, x_next[0], x_far[0]))
    own.scatter(4)
    nxt.tokens((3, 4), x_next[0], x_far[0])
    nxt.scatter(4)
    own.scatter(3)
    nxt.tokens((0, 1, 2), after(x_next[1], own.came), after(x_far[1], own.came))

    sent = own.scatter(2)
    nxt.scatter(3)
    sent = nxt.scatter(2, sent)

    grad_hidden = after(grad_hidden, sent).reshape(RING, 2, part, hidden // 4)
    grad_hidden = jnp.where(z // 2 % 2 == 0, grad_hidden, grad_hidden[:, ::-1])
    grad_hidden = grad_hidden.reshape(ROWS, part, hidden // 4)
    came = lax.all_to_all(grad_hidden, "row", 0, 0)
    sent = own.scatter(1)
    came = after(came.reshape(4, 4, part, hidden // 4), nxt.came)
    gates = []
    for m in range(DEPTHS):
        gate = lax.dynamic_index_in_dim(came, depth ^ m, 0, keepdims=False)
        gate = along_depth(gate, m) if m else gate
        gates.append(gate)
    nxt.scatter(1, own.at_home(), nxt.at_home(), sent)
    own.exchange()
    nxt.exchange()
    nxt.slope(gates[2:])
    own.slope(gates[:2], nxt.held[0])
    for j in range(4):
        nxt.gather()
        own.gather()

    def to_owner(result):
        return along_depth(result.astype(bf16), 2).astype(f32)

    parts = [own.product((1, 2)), nxt.product((0, 1, 2), own.held[3])]
    back = [to_owner(parts[1][2])]
    parts += [nxt.product((3,)), own.product((0, 3), nxt.held[3])]
    back += [to_owner(parts[2][2])]
    parts += [nxt.product((4,)), own.product((4,))]
    back += [to_owner(parts[4][2])]
    result = [parts[0][2] + back[0][slot:]]
    result += [jnp.concatenate([parts[3][2], parts[5][2]])]
    result[1] = result[1] + jnp.concatenate([back[0][:slot]] + back[1:])
    result = [r.astype(bf16) for r in result]

    result = jnp.stack(result).reshape(2, COLS, slot, width)
    pieces = [
        lax.dynamic_index_in_dim(result, (col + i) % COLS, 1, keepdims=False) for i in range(COLS)
    ]
    came = [pieces[0]] + [along_y(pieces[i], i) for i in range(1, COLS)]

    x_all = jnp.concatenate([p[0] for p in parts])
    grads = after(jnp.concatenate([p[1] for p in parts]), *pieces[1:])
    theirs = matmul(x_all, quarter(grads, 1 - core), ((0,), (0,))).astype(bf16)
    grad_weight = matmul(x_all, quarter(grads, core), ((0,), (0,)))
    came[0], grad_weight = lax.optimization_barrier((after(came[0], theirs), grad_weight))
    theirs = other_core(theirs).astype(f32)
    total = sum(c.astype(f32) for c in came).astype(bf16)

    mine = jnp.stack([total[:, :part], other_core(total[:, part:])], axis=1)
    around = jnp.stack([mine] + [along_y(mine, -i) for i in range(1, COLS)])
    grad_weight = (grad_weight + theirs).astype(bf16)
    around = rolled(around, (COLS - col) % COLS)
    sides = [[around[y, n] for y in range(COLS)] for n in range(2)]
    (one_f, one_s, two_f, two_s), (nil_f, three_f, three_s, four_f) = sides

    def side(x, c):
        return jnp.where(core == c, x[0], x[1])

    pairs = [(side(nil_f, 0), side(nil_f, 1))]
    pairs += [(side(f, 0), side(s, 0)) for f, s in ((one_f, one_s), (two_f, two_s), (three_f, three_s))]
    pairs += [(side(four_f, 0), side(four_f, 1))]
    pairs += [(side(s, 1), side(f, 1)) for f, s in ((three_f, three_s), (two_f, two_s), (one_f, one_s))]
    result = jnp.stack([jnp.stack(p) for p in pairs])
    result = rolled(result, (RING - z) % RING)
    result = jnp.where(half == 0, result, result[:, ::-1])
    return (result.reshape(tokens, width), grad_weight)


def solution(mesh):
    placed = (P("depth", "row"), P("row", "col"), P("depth", ("col", "row")))
    return jax.shard_map(
        body,
        mesh=mesh,
        in_specs=placed,
        out_specs=(P("depth", "row"), P("row", ("col", "depth"))),
        check_vma=False,
    )
```

```python
import math

import jax
import jax.numpy as jnp
from jax import lax
from jax.sharding import PartitionSpec as P

GELU_FACTOR = math.sqrt(2.0 / math.pi)
GELU_CUBIC = 0.044715

ROWS, COLS, DEPTHS = 16, 4, 4
RING = 8
AXES = ("row", "col", "depth")


def gelu_slope(values):
    argument = GELU_FACTOR * (values + GELU_CUBIC * values * values * values)
    tangent = jnp.tanh(argument)
    return 0.5 * (1.0 + tangent) + 0.5 * values * (1.0 - tangent * tangent) * GELU_FACTOR * (
        1.0 + 3.0 * GELU_CUBIC * values * values
    )


def send(x, target):
    perm = []
    for r in range(ROWS):
        for c in range(COLS):
            for d in range(DEPTHS):
                tz, th, tc, td = target(r // 2, r % 2, c, d)
                dst = (((tz % RING) * 2 + th) * COLS + tc % COLS) * DEPTHS + td
                perm.append(((r * COLS + c) * DEPTHS + d, dst))
    return lax.ppermute(x, AXES, perm)


def along_ring(x, back=False):
    return send(x, lambda z, h, y, d: (z + (1 if d % 2 == int(back) else -1), h, y, d))


def other_half(x):
    return send(x, lambda z, h, y, d: (z, 1 - h, y, d))


def along_y(x, step):
    return send(x, lambda z, h, y, d: (z, h, y + step, d))


def along_depth(x, mask):
    return send(x, lambda z, h, y, d: (z, h, y, d ^ mask))


def other_core(x):
    return along_depth(x, 1)


def rolled(x, shift):
    n = x.shape[0]
    return lax.dynamic_slice_in_dim(jnp.concatenate([x, x]), shift, n, 0)


def matmul(a, b, dims):
    return lax.dot_general(a, b, (dims, ((), ())), preferred_element_type=jnp.float32)


def after(x, *others):
    return lax.optimization_barrier((x, *others))[0]


def body(inputs, up_weight, grad_hidden):
    row, col, depth = (lax.axis_index(name) for name in AXES)
    z, half, core = row // 2, row % 2, depth % 2
    tokens, width = inputs.shape
    part = tokens // ROWS
    slot = 2 * part
    hidden = up_weight.shape[1] // DEPTHS
    f32, bf16 = jnp.float32, jnp.bfloat16

    def swapped(x):
        return jnp.concatenate([x[i * part : (i + 1) * part] for i in (3, 2, 1, 0)])

    x = inputs.reshape(RING, 2, part, width)
    x = rolled(jnp.where(half == 0, x, x[:, ::-1]), z)
    x_up = x[:5]
    x_down = jnp.stack([x[-j % RING, ::-1] for j in range(5)])
    x_mine = jnp.where(core == 0, x_up, x_down)
    x_other = jnp.where(core == 0, x_down, x_up)
    x_core = other_core(x_other)
    x_next, x_far = [
        [along_depth(x[piece], mask) for piece in (slice(3, 5), slice(0, 3))]
        for x, mask in ((x_mine, 2), (x_other, 3))
    ]

    weight = lax.dynamic_slice_in_dim(up_weight, depth // 2 * 2 * hidden, 2 * hidden, 1)
    weight = lax.optimization_barrier(weight)

    def quarter(x, c):
        return lax.dynamic_slice_in_dim(x, c * hidden, hidden, 1)

    class Stream:
        def __init__(self):
            self.x = [None] * 5

        def tokens(self, slots, first, second):
            x = jnp.stack([first, second], axis=2)
            for i, j in enumerate(slots):
                self.x[j] = x[i].reshape(2 * slot, width)

        def scatter(self, j, *others):
            if j == 4:
                sent = matmul(self.x[4][:slot], weight, ((1,), (0,))).astype(bf16)
                self.came = along_ring(sent)
            else:
                came = self.came.astype(f32)
                if j == 3:
                    came = jnp.concatenate([came, jnp.zeros_like(came)])
                x = after(self.x[j], *others) if others else self.x[j]
                sent = (matmul(x, weight, ((1,), (0,))) + came).astype(bf16)
                self.came = along_ring(sent)
            return sent

        def exchange(self):
            self.swap = other_core(swapped(quarter(self.came, 1 - core)))

        def at_home(self):
            home = matmul(self.x[0], quarter(weight, core), ((1,), (0,)))
            self.home = lax.optimization_barrier(home)
            return self.home

        def slope(self, gates, *others):
            total = self.home + quarter(self.came, core).astype(f32) + self.swap.astype(f32)
            total = total[:slot] + other_half(total[slot:].astype(bf16)).astype(f32)
            gates = [after(g, self.swap) for g in gates]
            gate = jnp.concatenate([g.transpose(1, 0, 2).reshape(part, hidden) for g in gates])
            grad = (gate.astype(f32) * gelu_slope(total)).astype(bf16)
            both = jnp.concatenate([grad, other_half(grad)])
            theirs = other_core(both)
            if others:
                theirs = after(theirs, *others)
            others = swapped(theirs)
            self.held = [
                jnp.where(
                    core == 0,
                    jnp.concatenate([both, others], axis=1),
                    jnp.concatenate([others, both], axis=1),
                )
            ]

        def gather(self):
            ahead = self.held[-1]
            if len(self.held) == 4:
                ahead = ahead[:slot]
            self.held.append(along_ring(ahead, back=True))

        def product(self, slots, *others):
            held = [self.held[j][:slot] if j in (0, 4) else self.held[j] for j in slots]
            x = [self.x[j][:slot] if j in (0, 4) else self.x[j] for j in slots]
            grads = jnp.concatenate([after(held[0], *others)] + held[1:])
            result = lax.optimization_barrier(matmul(grads, weight, ((1,), (1,))))
            return jnp.concatenate(x), grads, result

    own, nxt = Stream(), Stream()
    own.tokens(range(5), x_mine, after(x_core, x_next[0], x_far[0]))
    own.scatter(4)
    nxt.tokens((3, 4), x_next[0], x_far[0])
    nxt.scatter(4)
    own.scatter(3)
    nxt.tokens((0, 1, 2), after(x_next[1], own.came), after(x_far[1], own.came))

    sent = own.scatter(2)
    nxt.scatter(3)
    sent = nxt.scatter(2, sent)

    grad_hidden = after(grad_hidden, sent).reshape(RING, 2, part, hidden // 4)
    grad_hidden = jnp.where(z // 2 % 2 == 0, grad_hidden, grad_hidden[:, ::-1])
    grad_hidden = grad_hidden.reshape(ROWS, part, hidden // 4)
    came = lax.all_to_all(grad_hidden, "row", 0, 0)
    sent = own.scatter(1)
    came = after(came.reshape(4, 4, part, hidden // 4), nxt.came)
    gates = []
    for m in range(DEPTHS):
        gate = lax.dynamic_index_in_dim(came, depth ^ m, 0, keepdims=False)
        gate = along_depth(gate, m) if m else gate
        gates.append(gate)
    nxt.scatter(1, own.at_home(), nxt.at_home(), sent)
    own.exchange()
    nxt.exchange()
    nxt.slope(gates[2:])
    own.slope(gates[:2])
    for j in range(4):
        nxt.gather()
        own.gather()

    def to_owner(result):
        return along_depth(result.astype(bf16), 2).astype(f32)

    parts = [own.product((1, 2)), nxt.product((0, 1, 2), own.held[3])]
    back = [to_owner(parts[1][2])]
    parts += [nxt.product((3,)), own.product((0, 3), nxt.held[3])]
    back += [to_owner(parts[2][2])]
    parts += [nxt.product((4,)), own.product((4,))]
    back += [to_owner(parts[4][2])]
    result = [parts[0][2] + back[0][slot:]]
    result += [jnp.concatenate([parts[3][2], parts[5][2]])]
    result[1] = result[1] + jnp.concatenate([back[0][:slot]] + back[1:])
    result = [r.astype(bf16) for r in result]

    result = jnp.stack(result).reshape(2, COLS, slot, width)
    pieces = [
        lax.dynamic_index_in_dim(result, (col + i) % COLS, 1, keepdims=False) for i in range(COLS)
    ]
    came = [pieces[0]] + [along_y(pieces[i], i) for i in range(1, COLS)]

    x_all = jnp.concatenate([p[0] for p in parts])
    grads = after(jnp.concatenate([p[1] for p in parts]), *pieces[1:])
    theirs = matmul(x_all, quarter(grads, 1 - core), ((0,), (0,))).astype(bf16)
    grad_weight = matmul(x_all, quarter(grads, core), ((0,), (0,)))
    came[0], grad_weight = lax.optimization_barrier((after(came[0], theirs), grad_weight))
    theirs = other_core(theirs).astype(f32)
    total = sum(c.astype(f32) for c in came).astype(bf16)

    mine = jnp.stack([total[:, :part], other_core(total[:, part:])], axis=1)
    around = jnp.stack([mine] + [along_y(mine, -i) for i in range(1, COLS)])
    grad_weight = (grad_weight + theirs).astype(bf16)
    around = rolled(around, (COLS - col) % COLS)
    sides = [[around[y, n] for y in range(COLS)] for n in range(2)]
    (one_f, one_s, two_f, two_s), (nil_f, three_f, three_s, four_f) = sides

    def side(x, c):
        return jnp.where(core == c, x[0], x[1])

    pairs = [(side(nil_f, 0), side(nil_f, 1))]
    pairs += [(side(f, 0), side(s, 0)) for f, s in ((one_f, one_s), (two_f, two_s), (three_f, three_s))]
    pairs += [(side(four_f, 0), side(four_f, 1))]
    pairs += [(side(s, 1), side(f, 1)) for f, s in ((three_f, three_s), (two_f, two_s), (one_f, one_s))]
    result = jnp.stack([jnp.stack(p) for p in pairs])
    result = rolled(result, (RING - z) % RING)
    result = jnp.where(half == 0, result, result[:, ::-1])
    return (result.reshape(tokens, width), grad_weight)


def solution(mesh):
    placed = (P("depth", "row"), P("row", "col"), P("depth", ("col", "row")))
    return jax.shard_map(
        body,
        mesh=mesh,
        in_specs=placed,
        out_specs=(P("depth", "row"), P("row", ("col", "depth"))),
        check_vma=False,
    )
```
